32 devices in a mesh: seq: 8 (over z, y), head: 4 (over x, core).
Axes of the slice: x: 2, y: 2, z: 4, core: 2. Of those that a mesh axis runs over, the one named last changes fastest.
Arguments:
- queries: bfloat16 [1024, 1024], P('seq', 'head'), may hold values from -16 to 16
- key_vectors: bfloat16 [1024, 1024], P('seq', 'head'), may hold values from -16 to 16
- values: bfloat16 [1024, 1024], P('seq', 'head'), may hold values from -6 to 6
- step_rates: float32 [1024, 4], P('seq', 'head'), may hold values from 0.1 to 1
- fast_weights: float32 [4, 3, 256, 256], P('head', None, 'seq'), may hold values from -0.375 to 0.375
- momentum: float32 [4, 3, 256, 256], P('head', None, 'seq'), may hold values from -0.4375 to 0.4375
- momentum_decay: float32 [4], P('head'), may hold values from 0.5 to 0.95
- memory_gain: float32 [1024], P('head'), may hold values from 0.5 to 1.5
- window_gain: float32 [1024], P('head'), may hold values from 0.5 to 1.5
Outputs:
- blended: bfloat16 [1024, 1024], P('seq', 'head')
- new_weights: float32 [4, 3, 256, 256], P('head', None, 'seq')
- new_momentum: float32 [4, 3, 256, 256], P('head', None, 'seq')
The draws below stay inside these ranges and needn't reach their ends.
All inputs are finite; a program needn't handle non-finite values.
Results may differ from the reference program's by a relative error of at most 0.0085.
Values may be sent and summed in bfloat16 or wider, within the bound.
A program may use at most 64 MiB of HBM per device.

```python
import math
import jax
import jax.numpy as jnp
from jax import lax

DH = 256
HEADS = 4
WINDOW = 512
TOK_DEV = 128
TOKENS = 1024
D = 1024


def drawn_pair(key):
    base_key = jax.random.fold_in(key, 11)
    key_one, key_two = jax.random.split(base_key, 2)
    full_shape = (TOKENS, HEADS * DH)
    query_draw = jax.random.truncated_normal(key_one, -6.0, 6.0, full_shape, jnp.float32)
    key_draw = jax.random.truncated_normal(key_two, -6.0, 6.0, full_shape, jnp.float32)
    return (query_draw, key_draw)


def draw_queries(key, part):
    return drawn_pair(key)[0].astype(jnp.bfloat16)


def draw_key_vectors(key, part):
    return drawn_pair(key)[1].astype(jnp.bfloat16)


def block_scale(rng, dims, shards, smallest, high):
    def one(position, shards_of):
        steps = jax.random.uniform(jax.random.fold_in(jax.random.fold_in(rng, 6), position), (shards_of,), jnp.float32, smallest / len(shards), high / len(shards))
        return jnp.repeat(jnp.exp(steps), dims[position] // shards_of).reshape((-1,) + (1,) * (len(dims) - position - 1))

    level = one(*shards[0])
    for cut in shards[1:]:
        level = level * one(*cut)
    return level


def noise(stream_key, extent, deviation, limit, cuts=(), held_as=jnp.bfloat16):
    loudness = block_scale(stream_key, extent, cuts, -0.22, 0.18) if cuts else 1.0
    values = jax.random.normal(stream_key, extent, jnp.float32) * deviation * loudness
    return jnp.minimum(jnp.maximum(values, -limit), limit).astype(held_as)


def setup_inputs(seed: int = 0) -> dict:
    streams_of = jax.random.split(jax.random.key(seed), 10)
    return {
        "queries": draw_queries(jax.random.fold_in(streams_of[9], 71), 0),
        "key_vectors": draw_key_vectors(jax.random.fold_in(streams_of[9], 71), 0),
        "values": noise(streams_of[2], (TOKENS, D), 1.0, 6.0, ((0, 8), (1, 4))),
        "step_rates": jnp.clip(jnp.exp(math.log(1.0) - 2.3025851 * jax.random.uniform(streams_of[3], (TOKENS, HEADS), jnp.float32) ** block_scale(streams_of[3], (TOKENS, HEADS), ((0, 8), (1, 4)), -0.2, 0.2)), 0.1, 1.0),
        "fast_weights": noise(streams_of[4], (HEADS, 3, DH, DH), DH ** -0.5, 0.375, ((0, 4), (2, 8)), jnp.float32),
        "momentum": noise(streams_of[5], (HEADS, 3, DH, DH), 0.03, 0.4375, ((0, 4), (2, 8)), jnp.float32),
        "momentum_decay": jnp.clip(0.5 + 0.45 * jax.random.uniform(streams_of[6], (HEADS,), jnp.float32) ** block_scale(streams_of[6], (HEADS,), ((0, 4),), -0.2, 0.2), 0.5, 0.95),
        "memory_gain": jnp.clip(1.0 + 0.1 * jax.random.normal(streams_of[7], (D,), jnp.float32), 0.5, 1.5),
        "window_gain": jnp.clip(1.0 + 0.1 * jax.random.normal(streams_of[8], (D,), jnp.float32), 0.5, 1.5),
    }


def silu_slope(field):
    sigmoid_x = jax.nn.sigmoid(field)
    return sigmoid_x * (1.0 + field * (1.0 - sigmoid_x))

def keep_scale(candidate, previous):
    old_rms = jnp.sqrt(lax.optimization_barrier(jnp.mean(previous * previous, axis=-1, keepdims=True)) + 1e-06)
    new_rms = jnp.sqrt(lax.optimization_barrier(jnp.mean(candidate * candidate, axis=-1, keepdims=True)) + 1e-06)
    return candidate * (old_rms / new_rms)

def rms_scale(field, gain):
    return field * lax.rsqrt(lax.optimization_barrier(jnp.mean(field * field, axis=-1, keepdims=True)) + 1e-06) * gain

def window_attention(query_part, key_part, value_part):
    padded_keys = jnp.concatenate([jnp.zeros((WINDOW, DH), key_part.dtype), key_part], axis=0)
    padded_values = jnp.concatenate([jnp.zeros((WINDOW, DH), value_part.dtype), value_part], axis=0)
    block_count = TOKENS // TOK_DEV

    def one_block(block):
        first_row = (block * TOK_DEV).astype(jnp.int32)
        query_rows = lax.dynamic_slice_in_dim(query_part, first_row, TOK_DEV, 0)
        key_rows = lax.dynamic_slice_in_dim(padded_keys, first_row, TOK_DEV + WINDOW, 0)
        value_rows = lax.dynamic_slice_in_dim(padded_values, first_row, TOK_DEV + WINDOW, 0)
        scores = jnp.dot(query_rows, key_rows.T, preferred_element_type=jnp.float32) * DH ** (-0.5)
        query_pos = first_row + jnp.arange(TOK_DEV, dtype=jnp.int32)
        key_pos = first_row - WINDOW + jnp.arange(TOK_DEV + WINDOW, dtype=jnp.int32)
        distance = query_pos[:, None] - key_pos[None, :]
        allowed = (key_pos[None, :] >= 0) & (distance >= 0) & (distance < WINDOW)
        scores = jnp.where(allowed, scores, jnp.float32(-1e+30))
        row_max = lax.optimization_barrier(jnp.max(scores, axis=1, keepdims=True))
        weights = jnp.exp(scores - row_max)
        probabilities = (weights / lax.optimization_barrier(jnp.sum(weights, axis=1, keepdims=True))).astype(jnp.bfloat16)
        return jnp.dot(probabilities, value_rows, preferred_element_type=jnp.float32)
    blocks = lax.map(one_block, jnp.arange(block_count, dtype=jnp.int32))
    return blocks.reshape(TOKENS, DH)

def reference(queries, key_vectors, values, step_rates, fast_weights, momentum, momentum_decay, memory_gain, window_gain):
    inner_rate = 0.1 / math.sqrt(TOKENS)
    blended_heads = []
    weight_list = []
    moment_list = []
    for head_index in range(HEADS):
        low = head_index * DH
        query_part = queries[:, low:low + DH]
        key_part = key_vectors[:, low:low + DH]
        value_part = values[:, low:low + DH]
        rate_col = step_rates[:, head_index:head_index + 1]
        current = fast_weights[head_index]
        current_b = current.astype(jnp.bfloat16)
        gate_pre = jnp.dot(key_part, current_b[0], preferred_element_type=jnp.float32)
        up_pre = jnp.dot(key_part, current_b[1], preferred_element_type=jnp.float32)
        gate_act = jax.nn.silu(gate_pre)
        hidden = (gate_act * up_pre).astype(jnp.bfloat16)
        target_grad = (-(inner_rate * rate_col) * value_part.astype(jnp.float32)).astype(jnp.bfloat16)
        hidden_grad = jnp.dot(target_grad, current_b[2].T, preferred_element_type=jnp.float32)
        gate_grad = (hidden_grad * up_pre * silu_slope(gate_pre)).astype(jnp.bfloat16)
        up_grad = (hidden_grad * gate_act).astype(jnp.bfloat16)
        gradient = jnp.stack([jnp.dot(key_part.T, gate_grad, preferred_element_type=jnp.float32), jnp.dot(key_part.T, up_grad, preferred_element_type=jnp.float32), jnp.dot(hidden.T, target_grad, preferred_element_type=jnp.float32)])
        moment_new = momentum_decay[head_index] * momentum[head_index] + gradient
        weight_new = keep_scale(current - moment_new, current)
        updated = weight_new.astype(jnp.bfloat16)
        gate_out = jnp.dot(query_part, updated[0], preferred_element_type=jnp.float32)
        up_out = jnp.dot(query_part, updated[1], preferred_element_type=jnp.float32)
        inner_act = (jax.nn.silu(gate_out) * up_out).astype(jnp.bfloat16)
        recalled = jnp.dot(inner_act, updated[2], preferred_element_type=jnp.float32)
        attended = window_attention(query_part, key_part, value_part)
        joined = rms_scale(recalled, memory_gain[low:low + DH]) + rms_scale(attended, window_gain[low:low + DH])
        blended_heads.append(joined.astype(jnp.bfloat16))
        weight_list.append(weight_new)
        moment_list.append(moment_new)
    return (jnp.concatenate(blended_heads, axis=1), jnp.stack(weight_list), jnp.stack(moment_list))
```

```python
import functools
import math

import jax
import jax.numpy as jnp
from jax import lax
from jax.experimental import pallas as pl
from jax.experimental.pallas import tpu as pltpu
from jax.sharding import PartitionSpec as P

WINDOW = 512


def passed_along(value, axis, steps):
    count = lax.axis_size(axis)
    leading, last = (max(0, -steps), min(count, count - steps))
    return lax.ppermute(value, axis, [(source, source + steps) for source in range(leading, last)])


def silu_slope(field):
    sigmoid_x = jax.nn.sigmoid(field)
    return sigmoid_x * (1.0 + field * (1.0 - sigmoid_x))


def keep_scale(candidate, previous):
    old_rms = jnp.sqrt(jnp.mean(previous * previous, axis=-1, keepdims=True) + 1e-06)
    new_rms = jnp.sqrt(jnp.mean(candidate * candidate, axis=-1, keepdims=True) + 1e-06)
    return candidate * (old_rms / new_rms)


def rms_scale(field, gain):
    return field * lax.rsqrt(jnp.mean(field * field, axis=-1, keepdims=True) + 1e-06) * gain


def contract_rows(left, right):
    return lax.dot_general(
        left, right, (((0,), (0,)), ((), ())), preferred_element_type=jnp.float32
    )


def per_device(
    queries,
    key_vectors,
    values,
    step_rates,
    fast_weights,
    momentum,
    momentum_decay,
    memory_gain,
    window_gain,
):
    tokens_here, head_width = queries.shape
    seq_count = lax.axis_size("seq")
    my_index = lax.axis_index("seq")
    shard_rows = fast_weights.shape[2]
    inner_rate = 0.1 / math.sqrt(tokens_here * seq_count)
    hop_count = -(-WINDOW // tokens_here)
    border = (key_vectors, values)
    earlier = []
    for step_back in range(hop_count):
        earlier.append(passed_along((border[0], border[1]), "seq", step_back + 1))
    context_keys = jnp.concatenate(
        [piece[0] for piece in reversed(earlier)] + [key_vectors], axis=0
    )
    context_values = jnp.concatenate([piece[1] for piece in reversed(earlier)] + [values], axis=0)
    block_rows = min(tokens_here, max(WINDOW, 512))
    scores = lax.dot_general(
        queries, context_keys, (((1,), (1,)), ((), ())), preferred_element_type=jnp.float32
    ) * head_width ** (-0.5)
    query_pos = my_index * tokens_here + 0 + jnp.arange(block_rows, dtype=jnp.int32)
    key_pos = my_index * tokens_here + 0 - WINDOW + jnp.arange(block_rows + WINDOW, dtype=jnp.int32)
    distance = query_pos[:, None] - key_pos[None, :]
    allowed = (key_pos[None, :] >= 0) & (distance >= 0) & (distance < WINDOW)
    scores = jnp.where(allowed, scores, jnp.float32(-1e30))
    row_max = jnp.max(scores, axis=1, keepdims=True)
    weights = jnp.exp(scores - row_max)
    probabilities = (weights / jnp.sum(weights, axis=1, keepdims=True)).astype(jnp.bfloat16)
    attended_blocks = jnp.dot(probabilities, context_values, preferred_element_type=jnp.float32)
    owned = fast_weights[0]
    whole_weights, whole_moment = (
        lax.all_gather(owned, "seq", axis=1, tiled=True),
        lax.all_gather(momentum[0], "seq", axis=1, tiled=True),
    )
    gathered = whole_weights.astype(jnp.bfloat16)
    gate_pre = jnp.dot(key_vectors, gathered[0], preferred_element_type=jnp.float32)
    up_pre = jnp.dot(key_vectors, gathered[1], preferred_element_type=jnp.float32)
    gate_act = jax.nn.silu(gate_pre)
    hidden = (gate_act * up_pre).astype(jnp.bfloat16)
    target_grad = (-(inner_rate * step_rates) * values.astype(jnp.float32)).astype(jnp.bfloat16)
    hidden_grad = lax.dot_general(
        target_grad, gathered[2], (((1,), (1,)), ((), ())), preferred_element_type=jnp.float32
    )
    gate_grad = (hidden_grad * up_pre * silu_slope(gate_pre)).astype(jnp.bfloat16)
    up_grad = (hidden_grad * gate_act).astype(jnp.bfloat16)
    paired = jnp.concatenate([gate_grad, up_grad], axis=1)
    summed_all = lax.psum(
        jnp.concatenate(
            [contract_rows(key_vectors, paired), contract_rows(hidden, target_grad)], axis=1
        ),
        "seq",
    )
    gradient = summed_all.reshape(head_width, 3, head_width).transpose(1, 0, 2)
    moment_full = momentum_decay[0] * whole_moment + gradient
    weight_full = keep_scale(whole_weights - moment_full, whole_weights)
    updated = weight_full.astype(jnp.bfloat16)
    weight_new = lax.dynamic_slice_in_dim(weight_full, my_index * shard_rows, shard_rows, 1)
    moment_new = lax.dynamic_slice_in_dim(moment_full, my_index * shard_rows, shard_rows, 1)
    gate_out = jnp.dot(queries, updated[0], preferred_element_type=jnp.float32)
    up_out = jnp.dot(queries, updated[1], preferred_element_type=jnp.float32)
    inner_act = (jax.nn.silu(gate_out) * up_out).astype(jnp.bfloat16)
    recalled = jnp.dot(inner_act, updated[2], preferred_element_type=jnp.float32)
    blended = (rms_scale(recalled, memory_gain) + rms_scale(attended_blocks, window_gain)).astype(
        jnp.bfloat16
    )
    return (blended, weight_new[None], moment_new[None])


MESH = pl.DeviceIdType.MESH


def fused_kernel(
    count,
    q_ref,
    k_ref,
    v_ref,
    r_ref,
    w_ref,
    m_ref,
    decay_ref,
    mgain_ref,
    wgain_ref,
    out_ref,
    nw_ref,
    nm_ref,
    wg,
    ng,
    kv,
    rates,
    gpart,
    gin,
    send_sems,
    recv_sems,
):
    lines = count // 2
    tokens, width = q_ref.shape
    rows = w_ref.shape[2]
    me = lax.axis_index("seq")
    z, y = me // 2, me % 2
    partner = 2 * z + (1 - y)
    inner_rate = 0.1 / math.sqrt(tokens * count)
    used = {"send": 0}
    pending = []

    def line_peer(step):
        return 2 * lax.rem(z + step, lines) + y

    def copy_to(src, dst, recv, device):
        index = used["send"]
        used["send"] += 1
        return pltpu.make_async_remote_copy(
            src_ref=src,
            dst_ref=dst,
            send_sem=send_sems.at[index],
            recv_sem=recv_sems.at[recv],
            device_id={"seq": device},
            device_id_type=MESH,
        )

    def start(src, dst, recv, device, when=None):
        copy = copy_to(src, dst, recv, device)
        pending.append((copy, when))
        if when is None:
            copy.start()
        else:
            pl.when(when)(copy.start)

    def arrived(dst, recv, when=None):
        copy = pltpu.make_async_remote_copy(
            src_ref=dst,
            dst_ref=dst,
            send_sem=send_sems.at[0],
            recv_sem=recv_sems.at[recv],
            device_id={"seq": partner},
            device_id_type=MESH,
        )
        if when is None:
            copy.wait_recv()
        else:
            pl.when(when)(copy.wait_recv)

    def row_block(buffer, device):
        return buffer.at[:, pl.ds(pl.multiple_of(device * rows, rows), rows), :]

    def slot(index):
        return kv.at[:, pl.ds(pl.multiple_of(index * tokens, tokens), tokens), :]

    W_LINE, W_PAIR = 0, lines
    N_LINE, N_PAIR = 2 * lines, 3 * lines
    G_LINE = 4 * lines
    KV_PAIR, RATE_PAIR, NEAR, FAR, NEAR_PAIR, FAR_PAIR = range(5 * lines, 5 * lines + 6)

    barrier = pltpu.get_barrier_semaphore()
    greeted = [partner] + [line_peer(step) for step in range(1, lines)]
    for device in greeted:
        pl.semaphore_signal(barrier, inc=1, device_id={"seq": device}, device_id_type=MESH)

    my_rows = pl.ds(pl.multiple_of(me * rows, rows), rows)
    wg[:, my_rows, :] = w_ref[0].astype(jnp.bfloat16)
    my_slot = pl.ds(pl.multiple_of((4 + y) * tokens, tokens), tokens)
    kv[0, my_slot, :] = k_ref[...]
    kv[1, my_slot, :] = v_ref[...]
    rates[y] = jnp.broadcast_to(r_ref[...], (tokens, 128)).T[:8]

    def clear(index):
        kv[:, index * tokens : (index + 1) * tokens, :] = jnp.zeros(
            (2, tokens, width), jnp.bfloat16
        )

    @pl.when(z < 2)
    def _():
        clear(0)
        clear(1)

    @pl.when(z < 1)
    def _():
        clear(2)
        clear(3)

    @pl.when((z >= 2) & (y == 1))
    def _():
        clear(0)

    pl.semaphore_wait(barrier, len(greeted))

    for step in range(1, lines):
        start(row_block(wg, me), row_block(wg, me), W_LINE + step, line_peer(step))
    start(row_block(wg, me), row_block(wg, me), W_PAIR, partner)
    start(rates.at[y], rates.at[y], RATE_PAIR, partner)
    start(slot(4 + y), slot(4 + y), KV_PAIR, partner)
    start(slot(4 + y), slot(2 + y), NEAR, 2 * (z + 1) + y, z + 1 < lines)

    def forwards(buffer, line, pair):
        for step in range(1, lines):
            origin = line_peer(lines - step)
            arrived(row_block(buffer, origin), line + step)
            start(row_block(buffer, origin), row_block(buffer, origin), pair + step, partner)

    def forwards_done(buffer, pair):
        for step in range(lines):
            origin = 2 * lax.rem(z + lines - step, lines) + (1 - y)
            arrived(row_block(buffer, origin), pair + step)

    forwards(wg, W_LINE, W_PAIR)
    arrived(rates.at[1 - y], RATE_PAIR)
    arrived(slot(5 - y), KV_PAIR)
    pair_keys = kv[0, 4 * tokens : 6 * tokens, :]
    pair_values = kv[1, 4 * tokens : 6 * tokens, :]
    rate_cols = []
    for index in range(2):
        column = jnp.broadcast_to(rates[index][0:1], (128, tokens)).T
        rate_cols.append(jnp.concatenate([column] * (width // 128), axis=1))
    rate_all = jnp.concatenate(rate_cols, axis=0)
    target_grad = (-(inner_rate * rate_all) * pair_values.astype(jnp.float32)).astype(
        jnp.bfloat16
    )
    forwards_done(wg, W_PAIR)
    gate_pre = jnp.dot(pair_keys, wg[0], preferred_element_type=jnp.float32)
    up_pre = jnp.dot(pair_keys, wg[1], preferred_element_type=jnp.float32)
    hidden_grad = lax.dot_general(
        target_grad, wg[2], (((1,), (1,)), ((), ())), preferred_element_type=jnp.float32
    )
    sigmoid_x = jax.nn.sigmoid(gate_pre)
    gate_act = gate_pre * sigmoid_x
    hidden = (gate_act * up_pre).astype(jnp.bfloat16)
    slope = sigmoid_x * (1.0 + gate_pre * (1.0 - sigmoid_x))
    gate_grad = (hidden_grad * up_pre * slope).astype(jnp.bfloat16)
    up_grad = (hidden_grad * gate_act).astype(jnp.bfloat16)
    gpart[0] = contract_rows(pair_keys, gate_grad).astype(jnp.bfloat16)
    gpart[1] = contract_rows(pair_keys, up_grad).astype(jnp.bfloat16)
    gpart[2] = contract_rows(hidden, target_grad).astype(jnp.bfloat16)
    for step in range(1, lines):
        device = line_peer(step)
        start(row_block(gpart, device), gin.at[step], G_LINE + step, device)

    near = z >= 1
    far = z >= 2
    arrived(slot(2 + y), NEAR, near)
    start(slot(2 + y), slot(y), FAR, 2 * (z + 1) + y, near & (z + 1 < lines))
    start(slot(2 + y), slot(2 + y), NEAR_PAIR, partner, near)

    old = w_ref[0]
    total = gpart[:, my_rows, :].astype(jnp.float32)
    for step in range(1, lines):
        arrived(gin.at[step], G_LINE + step)
        total += gin[step].astype(jnp.float32)
    moment = decay_ref[0] * m_ref[0] + total
    nm_ref[0] = moment
    fresh = keep_scale(old - moment, old)
    nw_ref[0] = fresh
    ng[:, my_rows, :] = fresh.astype(jnp.bfloat16)
    for step in range(1, lines):
        start(row_block(ng, me), row_block(ng, me), N_LINE + step, line_peer(step))
    start(row_block(ng, me), row_block(ng, me), N_PAIR, partner)

    arrived(slot(y), FAR, far)
    start(slot(1), slot(1), FAR_PAIR, partner, far & (y == 1))
    forwards(ng, N_LINE, N_PAIR)
    arrived(slot(3 - y), NEAR_PAIR, near)
    arrived(slot(1), FAR_PAIR, far & (y == 0))

    scores = lax.dot_general(
        q_ref[...], kv[0], (((1,), (1,)), ((), ())), preferred_element_type=jnp.float32
    ) * width ** (-0.5)
    shape = scores.shape
    key_index = lax.broadcasted_iota(jnp.int32, shape, 1)
    distance = (y + 4) * tokens + lax.broadcasted_iota(jnp.int32, shape, 0) - key_index
    key_pos = (2 * z - 4) * tokens + key_index
    allowed = (key_pos >= 0) & (distance >= 0) & (distance < WINDOW)
    scores = jnp.where(allowed, scores, jnp.float32(-1e30))
    weights = jnp.exp(scores - jnp.max(scores, axis=1, keepdims=True))
    probabilities = (weights / jnp.sum(weights, axis=1, keepdims=True)).astype(jnp.bfloat16)
    attended = jnp.dot(probabilities, kv[1], preferred_element_type=jnp.float32)
    attended = rms_scale(attended, wgain_ref[...])

    forwards_done(ng, N_PAIR)
    queries = q_ref[...]
    gate_out = jnp.dot(queries, ng[0], preferred_element_type=jnp.float32)
    up_out = jnp.dot(queries, ng[1], preferred_element_type=jnp.float32)
    inner_act = (jax.nn.silu(gate_out) * up_out).astype(jnp.bfloat16)
    recalled = jnp.dot(inner_act, ng[2], preferred_element_type=jnp.float32)
    out_ref[...] = (rms_scale(recalled, mgain_ref[...]) + attended).astype(jnp.bfloat16)

    for copy, when in pending:
        if when is None:
            copy.wait_send()
        else:
            pl.when(when)(copy.wait_send)


def fused(
    queries,
    key_vectors,
    values,
    step_rates,
    fast_weights,
    momentum,
    momentum_decay,
    memory_gain,
    window_gain,
):
    tokens, width = queries.shape
    count = lax.axis_size("seq")
    lines = count // 2
    vmem = pl.BlockSpec(memory_space=pltpu.VMEM)
    smem = pl.BlockSpec(memory_space=pltpu.SMEM)
    bf16 = jnp.bfloat16
    return pl.pallas_call(
        functools.partial(fused_kernel, count),
        out_shape=(
            jax.ShapeDtypeStruct(queries.shape, bf16),
            jax.ShapeDtypeStruct(fast_weights.shape, jnp.float32),
            jax.ShapeDtypeStruct(momentum.shape, jnp.float32),
        ),
        in_specs=[vmem] * 6 + [smem] + [vmem] * 2,
        out_specs=(vmem,) * 3,
        scratch_shapes=[
            pltpu.VMEM((3, width, width), bf16),
            pltpu.VMEM((3, width, width), bf16),
            pltpu.VMEM((2, 6 * tokens, width), bf16),
            pltpu.VMEM((2, 8, tokens), jnp.float32),
            pltpu.VMEM((3, width, width), bf16),
            pltpu.VMEM((lines,) + fast_weights.shape[1:], bf16),
            pltpu.SemaphoreType.DMA((5 * lines + 8,)),
            pltpu.SemaphoreType.DMA((5 * lines + 6,)),
        ],
        compiler_params=pltpu.CompilerParams(
            collective_id=0, has_side_effects=True, vmem_limit_bytes=32 * 1024 * 1024
        ),
    )(
        queries,
        key_vectors,
        values,
        step_rates,
        fast_weights,
        momentum,
        momentum_decay,
        memory_gain.reshape(1, width),
        window_gain.reshape(1, width),
    )


def layer(*args):
    tokens, width = args[0].shape
    count = lax.axis_size("seq")
    rows = args[4].shape[2]
    pairs = count % 2 == 0 and count >= 4
    if pairs and tokens == 128 and WINDOW == 4 * tokens and rows % 16 == 0 and width % 128 == 0:
        return fused(*args)
    return per_device(*args)


def solution(mesh):
    in_specs = (
        P("seq", "head"),
        P("seq", "head"),
        P("seq", "head"),
        P("seq", "head"),
        P("head", None, "seq", None),
        P("head", None, "seq", None),
        P("head"),
        P("head"),
        P("head"),
    )
    out_specs = (P("seq", "head"), P("head", None, "seq", None), P("head", None, "seq", None))
    return jax.shard_map(
        layer, mesh=mesh, in_specs=in_specs, out_specs=out_specs, check_vma=False
    )
```

```python
import functools
import math

import jax
import jax.numpy as jnp
from jax import lax
from jax.experimental import pallas as pl
from jax.experimental.pallas import tpu as pltpu
from jax.sharding import PartitionSpec as P

WINDOW = 512
VMEM_BYTES = 60 * 1024 * 1024


def passed_along(value, axis, steps):
    count = lax.axis_size(axis)
    leading, last = (max(0, -steps), min(count, count - steps))
    return lax.ppermute(value, axis, [(source, source + steps) for source in range(leading, last)])


def silu_slope(field):
    sigmoid_x = jax.nn.sigmoid(field)
    return sigmoid_x * (1.0 + field * (1.0 - sigmoid_x))


def keep_scale(candidate, previous):
    old_rms = jnp.sqrt(jnp.mean(previous * previous, axis=-1, keepdims=True) + 1e-06)
    new_rms = jnp.sqrt(jnp.mean(candidate * candidate, axis=-1, keepdims=True) + 1e-06)
    return candidate * (old_rms / new_rms)


def rms_scale(field, gain):
    return field * lax.rsqrt(jnp.mean(field * field, axis=-1, keepdims=True) + 1e-06) * gain


def contract_rows(left, right):
    return lax.dot_general(
        left, right, (((0,), (0,)), ((), ())), preferred_element_type=jnp.float32
    )


def per_device(
    queries,
    key_vectors,
    values,
    step_rates,
    fast_weights,
    momentum,
    momentum_decay,
    memory_gain,
    window_gain,
):
    tokens_here, head_width = queries.shape
    seq_count = lax.axis_size("seq")
    my_index = lax.axis_index("seq")
    shard_rows = fast_weights.shape[2]
    inner_rate = 0.1 / math.sqrt(tokens_here * seq_count)
    hop_count = -(-WINDOW // tokens_here)
    border = (key_vectors, values)
    earlier = []
    for step_back in range(hop_count):
        earlier.append(passed_along((border[0], border[1]), "seq", step_back + 1))
    context_keys = jnp.concatenate(
        [piece[0] for piece in reversed(earlier)] + [key_vectors], axis=0
    )
    context_values = jnp.concatenate([piece[1] for piece in reversed(earlier)] + [values], axis=0)
    block_rows = min(tokens_here, max(WINDOW, 512))
    scores = lax.dot_general(
        queries, context_keys, (((1,), (1,)), ((), ())), preferred_element_type=jnp.float32
    ) * head_width ** (-0.5)
    query_pos = my_index * tokens_here + 0 + jnp.arange(block_rows, dtype=jnp.int32)
    key_pos = my_index * tokens_here + 0 - WINDOW + jnp.arange(block_rows + WINDOW, dtype=jnp.int32)
    distance = query_pos[:, None] - key_pos[None, :]
    allowed = (key_pos[None, :] >= 0) & (distance >= 0) & (distance < WINDOW)
    scores = jnp.where(allowed, scores, jnp.float32(-1e30))
    row_max = jnp.max(scores, axis=1, keepdims=True)
    weights = jnp.exp(scores - row_max)
    probabilities = (weights / jnp.sum(weights, axis=1, keepdims=True)).astype(jnp.bfloat16)
    attended_blocks = jnp.dot(probabilities, context_values, preferred_element_type=jnp.float32)
    owned = fast_weights[0]
    whole_weights, whole_moment = (
        lax.all_gather(owned, "seq", axis=1, tiled=True),
        lax.all_gather(momentum[0], "seq", axis=1, tiled=True),
    )
    gathered = whole_weights.astype(jnp.bfloat16)
    gate_pre = jnp.dot(key_vectors, gathered[0], preferred_element_type=jnp.float32)
    up_pre = jnp.dot(key_vectors, gathered[1], preferred_element_type=jnp.float32)
    gate_act = jax.nn.silu(gate_pre)
    hidden = (gate_act * up_pre).astype(jnp.bfloat16)
    target_grad = (-(inner_rate * step_rates) * values.astype(jnp.float32)).astype(jnp.bfloat16)
    hidden_grad = lax.dot_general(
        target_grad, gathered[2], (((1,), (1,)), ((), ())), preferred_element_type=jnp.float32
    )
    gate_grad = (hidden_grad * up_pre * silu_slope(gate_pre)).astype(jnp.bfloat16)
    up_grad = (hidden_grad * gate_act).astype(jnp.bfloat16)
    paired = jnp.concatenate([gate_grad, up_grad], axis=1)
    summed_all = lax.psum(
        jnp.concatenate(
            [contract_rows(key_vectors, paired), contract_rows(hidden, target_grad)], axis=1
        ),
        "seq",
    )
    gradient = summed_all.reshape(head_width, 3, head_width).transpose(1, 0, 2)
    moment_full = momentum_decay[0] * whole_moment + gradient
    weight_full = keep_scale(whole_weights - moment_full, whole_weights)
    updated = weight_full.astype(jnp.bfloat16)
    weight_new = lax.dynamic_slice_in_dim(weight_full, my_index * shard_rows, shard_rows, 1)
    moment_new = lax.dynamic_slice_in_dim(moment_full, my_index * shard_rows, shard_rows, 1)
    gate_out = jnp.dot(queries, updated[0], preferred_element_type=jnp.float32)
    up_out = jnp.dot(queries, updated[1], preferred_element_type=jnp.float32)
    inner_act = (jax.nn.silu(gate_out) * up_out).astype(jnp.bfloat16)
    recalled = jnp.dot(inner_act, updated[2], preferred_element_type=jnp.float32)
    blended = (rms_scale(recalled, memory_gain) + rms_scale(attended_blocks, window_gain)).astype(
        jnp.bfloat16
    )
    return (blended, weight_new[None], moment_new[None])


MESH = pl.DeviceIdType.MESH


def fused_kernel(
    count,
    q_hbm,
    k_hbm,
    v_hbm,
    r_hbm,
    w_hbm,
    m_hbm,
    decay_hbm,
    mgain_hbm,
    wgain_hbm,
    out_hbm,
    nw_hbm,
    nm_hbm,
    out_ref,
    nw_ref,
    nm_ref,
    q_ref,
    w_ref,
    m_ref,
    decay_ref,
    mgain_ref,
    wgain_ref,
    local_sems,
    wg,
    ng,
    kv,
    rates,
    gpart,
    gin,
    send_sems,
    recv_sems,
):
    lines = count // 2
    tokens, width = q_ref.shape
    rows = w_ref.shape[2]
    me = lax.axis_index("seq")
    z, y = me // 2, me % 2
    partner = 2 * z + (1 - y)
    inner_rate = 0.1 / math.sqrt(tokens * count)
    used = {"send": 0}
    pending = []

    def line_peer(step):
        return 2 * lax.rem(z + step, lines) + y

    def copy_to(src, dst, recv, device):
        index = used["send"]
        used["send"] += 1
        return pltpu.make_async_remote_copy(
            src_ref=src,
            dst_ref=dst,
            send_sem=send_sems.at[index],
            recv_sem=recv_sems.at[recv],
            device_id={"seq": device},
            device_id_type=MESH,
        )

    def start(src, dst, recv, device, when=None):
        copy = copy_to(src, dst, recv, device)
        pending.append((copy, when))
        if when is None:
            copy.start()
        else:
            pl.when(when)(copy.start)

    def arrived(dst, recv, when=None):
        copy = pltpu.make_async_remote_copy(
            src_ref=dst,
            dst_ref=dst,
            send_sem=send_sems.at[0],
            recv_sem=recv_sems.at[recv],
            device_id={"seq": partner},
            device_id_type=MESH,
        )
        if when is None:
            copy.wait_recv()
        else:
            pl.when(when)(copy.wait_recv)

    def row_block(buffer, device):
        return buffer.at[:, pl.ds(pl.multiple_of(device * rows, rows), rows), :]

    def slot(index):
        return kv.at[:, pl.ds(pl.multiple_of(index * tokens, tokens), tokens), :]

    W_LINE, W_PAIR = 0, lines
    N_LINE, N_PAIR = 2 * lines, 3 * lines
    G_LINE = 4 * lines
    KV_PAIR, RATE_PAIR, NEAR, FAR, NEAR_PAIR, FAR_PAIR = range(5 * lines, 5 * lines + 6)

    barrier = pltpu.get_barrier_semaphore()
    greeted = [partner] + [line_peer(step) for step in range(1, lines)]
    for device in greeted:
        pl.semaphore_signal(barrier, inc=1, device_id={"seq": device}, device_id_type=MESH)

    my_rows = pl.ds(pl.multiple_of(me * rows, rows), rows)
    my_slot = pl.ds(pl.multiple_of((4 + y) * tokens, tokens), tokens)
    loads = [
        pltpu.make_async_copy(src, dst, local_sems.at[index])
        for index, (src, dst) in enumerate(
            (
                (w_hbm, w_ref),
                (r_hbm, rates.at[y]),
                (k_hbm, kv.at[0, my_slot, :]),
                (v_hbm, kv.at[1, my_slot, :]),
                (m_hbm, m_ref),
                (q_hbm, q_ref),
                (mgain_hbm, mgain_ref),
                (wgain_hbm, wgain_ref),
                (decay_hbm, decay_ref),
            )
        )
    ]
    for load in loads:
        load.start()

    def clear(index):
        kv[:, index * tokens : (index + 1) * tokens, :] = jnp.zeros(
            (2, tokens, width), jnp.bfloat16
        )

    @pl.when(z < 2)
    def _():
        clear(0)
        clear(1)

    @pl.when(z < 1)
    def _():
        clear(2)
        clear(3)

    @pl.when((z >= 2) & (y == 1))
    def _():
        clear(0)

    loads[0].wait()
    wg[:, my_rows, :] = w_ref[0].astype(jnp.bfloat16)
    pl.semaphore_wait(barrier, len(greeted))

    for step in range(1, lines):
        start(row_block(wg, me), row_block(wg, me), W_LINE + step, line_peer(step))
    start(row_block(wg, me), row_block(wg, me), W_PAIR, partner)
    for load in loads[1:4]:
        load.wait()
    start(rates.at[y], rates.at[y], RATE_PAIR, partner)
    start(slot(4 + y), slot(4 + y), KV_PAIR, partner)
    start(slot(4 + y), slot(2 + y), NEAR, 2 * (z + 1) + y, z + 1 < lines)

    def forwards(buffer, line, pair):
        for step in range(1, lines):
            origin = line_peer(lines - step)
            arrived(row_block(buffer, origin), line + step)
            start(row_block(buffer, origin), row_block(buffer, origin), pair + step, partner)

    def forwards_done(buffer, pair):
        for step in range(lines):
            origin = 2 * lax.rem(z + lines - step, lines) + (1 - y)
            arrived(row_block(buffer, origin), pair + step)

    forwards(wg, W_LINE, W_PAIR)
    arrived(rates.at[1 - y], RATE_PAIR)
    arrived(slot(5 - y), KV_PAIR)
    pair_keys = kv[0, 4 * tokens : 6 * tokens, :]
    pair_values = kv[1, 4 * tokens : 6 * tokens, :]
    rate_cols = []
    for index in range(2):
        column = jnp.broadcast_to(rates[index], (128, tokens)).T
        rate_cols.append(jnp.concatenate([column] * (width // 128), axis=1))
    rate_all = jnp.concatenate(rate_cols, axis=0)
    target_grad = (-(inner_rate * rate_all) * pair_values.astype(jnp.float32)).astype(
        jnp.bfloat16
    )
    forwards_done(wg, W_PAIR)
    gate_pre = jnp.dot(pair_keys, wg[0], preferred_element_type=jnp.float32)
    up_pre = jnp.dot(pair_keys, wg[1], preferred_element_type=jnp.float32)
    hidden_grad = lax.dot_general(
        target_grad, wg[2], (((1,), (1,)), ((), ())), preferred_element_type=jnp.float32
    )
    sigmoid_x = jax.nn.sigmoid(gate_pre)
    gate_act = gate_pre * sigmoid_x
    hidden = (gate_act * up_pre).astype(jnp.bfloat16)
    slope = sigmoid_x * (1.0 + gate_pre * (1.0 - sigmoid_x))
    gate_grad = (hidden_grad * up_pre * slope).astype(jnp.bfloat16)
    up_grad = (hidden_grad * gate_act).astype(jnp.bfloat16)
    gpart[0] = contract_rows(pair_keys, gate_grad).astype(jnp.bfloat16)
    gpart[1] = contract_rows(pair_keys, up_grad).astype(jnp.bfloat16)
    gpart[2] = contract_rows(hidden, target_grad).astype(jnp.bfloat16)
    for step in range(1, lines):
        device = line_peer(step)
        start(row_block(gpart, device), gin.at[step], G_LINE + step, device)

    near = z >= 1
    far = z >= 2
    arrived(slot(2 + y), NEAR, near)
    start(slot(2 + y), slot(y), FAR, 2 * (z + 1) + y, near & (z + 1 < lines))
    start(slot(2 + y), slot(2 + y), NEAR_PAIR, partner, near)

    for load in loads[4:]:
        load.wait()
    old = w_ref[0]
    total = gpart[:, my_rows, :].astype(jnp.float32)
    for step in range(1, lines):
        arrived(gin.at[step], G_LINE + step)
        total += gin[step].astype(jnp.float32)
    moment = decay_ref[0] * m_ref[0] + total
    nm_ref[0] = moment
    moment_copy = pltpu.make_async_copy(nm_ref, nm_hbm, local_sems.at[9])
    moment_copy.start()
    fresh = keep_scale(old - moment, old)
    nw_ref[0] = fresh
    ng[:, my_rows, :] = fresh.astype(jnp.bfloat16)
    for step in range(1, lines):
        start(row_block(ng, me), row_block(ng, me), N_LINE + step, line_peer(step))
    start(row_block(ng, me), row_block(ng, me), N_PAIR, partner)
    weight_copy = pltpu.make_async_copy(nw_ref, nw_hbm, local_sems.at[10])
    weight_copy.start()

    arrived(slot(y), FAR, far)
    start(slot(1), slot(1), FAR_PAIR, partner, far & (y == 1))
    forwards(ng, N_LINE, N_PAIR)
    arrived(slot(3 - y), NEAR_PAIR, near)
    arrived(slot(1), FAR_PAIR, far & (y == 0))

    scores = lax.dot_general(
        q_ref[...], kv[0], (((1,), (1,)), ((), ())), preferred_element_type=jnp.float32
    ) * width ** (-0.5)
    shape = scores.shape
    key_index = lax.broadcasted_iota(jnp.int32, shape, 1)
    distance = (y + 4) * tokens + lax.broadcasted_iota(jnp.int32, shape, 0) - key_index
    key_pos = (2 * z - 4) * tokens + key_index
    allowed = (key_pos >= 0) & (distance >= 0) & (distance < WINDOW)
    scores = jnp.where(allowed, scores, jnp.float32(-1e30))
    weights = jnp.exp(scores - jnp.max(scores, axis=1, keepdims=True))
    probabilities = (weights / jnp.sum(weights, axis=1, keepdims=True)).astype(jnp.bfloat16)
    attended = jnp.dot(probabilities, kv[1], preferred_element_type=jnp.float32)
    attended = rms_scale(attended, wgain_ref[...])

    forwards_done(ng, N_PAIR)
    queries = q_ref[...]
    gate_out = jnp.dot(queries, ng[0], preferred_element_type=jnp.float32)
    up_out = jnp.dot(queries, ng[1], preferred_element_type=jnp.float32)
    inner_act = (jax.nn.silu(gate_out) * up_out).astype(jnp.bfloat16)
    recalled = jnp.dot(inner_act, ng[2], preferred_element_type=jnp.float32)
    out_ref[...] = (rms_scale(recalled, mgain_ref[...]) + attended).astype(jnp.bfloat16)
    out_copy = pltpu.make_async_copy(out_ref, out_hbm, local_sems.at[11])
    out_copy.start()

    for copy, when in pending:
        if when is None:
            copy.wait_send()
        else:
            pl.when(when)(copy.wait_send)
    moment_copy.wait()
    weight_copy.wait()
    out_copy.wait()


def fused(
    queries,
    key_vectors,
    values,
    step_rates,
    fast_weights,
    momentum,
    momentum_decay,
    memory_gain,
    window_gain,
):
    tokens, width = queries.shape
    count = lax.axis_size("seq")
    lines = count // 2
    hbm = pl.BlockSpec(memory_space=pltpu.HBM)
    bf16 = jnp.bfloat16
    results = pl.pallas_call(
        functools.partial(fused_kernel, count),
        out_shape=(
            jax.ShapeDtypeStruct(queries.shape, bf16),
            jax.ShapeDtypeStruct(fast_weights.shape, jnp.float32),
            jax.ShapeDtypeStruct(momentum.shape, jnp.float32),
        ),
        in_specs=[hbm] * 9,
        out_specs=(hbm,) * 3,
        scratch_shapes=[
            pltpu.VMEM(queries.shape, bf16),
            pltpu.VMEM(fast_weights.shape, jnp.float32),
            pltpu.VMEM(momentum.shape, jnp.float32),
            pltpu.VMEM(queries.shape, bf16),
            pltpu.VMEM(fast_weights.shape, jnp.float32),
            pltpu.VMEM(momentum.shape, jnp.float32),
            pltpu.SMEM((1,), jnp.float32),
            pltpu.VMEM((1, width), jnp.float32),
            pltpu.VMEM((1, width), jnp.float32),
            pltpu.SemaphoreType.DMA((12,)),
            pltpu.VMEM((3, width, width), bf16),
            pltpu.VMEM((3, width, width), bf16),
            pltpu.VMEM((2, 6 * tokens, width), bf16),
            pltpu.VMEM((2, 1, tokens), jnp.float32),
            pltpu.VMEM((3, width, width), bf16),
            pltpu.VMEM((lines,) + fast_weights.shape[1:], bf16),
            pltpu.SemaphoreType.DMA((5 * lines + 8,)),
            pltpu.SemaphoreType.DMA((5 * lines + 6,)),
        ],
        compiler_params=pltpu.CompilerParams(
            collective_id=0, has_side_effects=True, vmem_limit_bytes=VMEM_BYTES
        ),
    )(
        queries,
        key_vectors,
        values,
        step_rates.reshape(1, tokens),
        fast_weights,
        momentum,
        momentum_decay,
        memory_gain.reshape(1, width),
        window_gain.reshape(1, width),
    )
    return store(results)


def store_kernel(*refs):
    sources, targets, held, sems = refs[:3], refs[3:6], refs[6:9], refs[9]
    loads = [
        pltpu.make_async_copy(src, mid, sems.at[index])
        for index, (src, mid) in enumerate(zip(sources, held))
    ]
    stores = [
        pltpu.make_async_copy(mid, dst, sems.at[3 + index])
        for index, (mid, dst) in enumerate(zip(held, targets))
    ]
    for load in loads:
        load.start()
    for load, copy in zip(loads, stores):
        load.wait()
        copy.start()
    for copy in stores:
        copy.wait()


def store(results):
    return pl.pallas_call(
        store_kernel,
        out_shape=tuple(jax.ShapeDtypeStruct(x.shape, x.dtype) for x in results),
        in_specs=[pl.BlockSpec(memory_space=pltpu.HBM)] * 3,
        out_specs=(pl.BlockSpec(memory_space=pltpu.HBM),) * 3,
        scratch_shapes=[pltpu.VMEM(x.shape, x.dtype) for x in results]
        + [pltpu.SemaphoreType.DMA((6,))],
        compiler_params=pltpu.CompilerParams(vmem_limit_bytes=VMEM_BYTES),
    )(*results)


def layer(*args):
    tokens, width = args[0].shape
    count = lax.axis_size("seq")
    rows = args[4].shape[2]
    pairs = count % 2 == 0 and count >= 4
    if pairs and tokens == 128 and WINDOW == 4 * tokens and rows % 16 == 0 and width % 128 == 0:
        return fused(*args)
    return per_device(*args)


def solution(mesh):
    in_specs = (
        P("seq", "head"),
        P("seq", "head"),
        P("seq", "head"),
        P("seq", "head"),
        P("head", None, "seq", None),
        P("head", None, "seq", None),
        P("head"),
        P("head"),
        P("head"),
    )
    out_specs = (P("seq", "head"), P("head", None, "seq", None), P("head", None, "seq", None))
    return jax.shard_map(
        layer, mesh=mesh, in_specs=in_specs, out_specs=out_specs, check_vma=False
    )
```
